32 devices in a mesh: groups: 2 (over y), uv: 4 (over z), tm: 2 (over x), chan: 2 (over core).
Axes of the slice: x: 2, y: 2, z: 4, core: 2. Of those that a mesh axis runs over, the one named last changes fastest.
Arguments:
- visibilities: bfloat16 [2, 4, 8192, 256], P(None, 'tm', ('groups', 'uv'), 'chan'), parts along dimension 2, may hold values from -6 to 6
- baseline_keep_mask: int32 [8192], P(('groups', 'uv')), parts along dimension 0, may hold values 0 or 1
- channel_flags: int32 [512], P(('groups', 'chan')), parts along dimension 0, may hold values 0 or 1
- baseline_spacing: float32 [2, 4, 8192], P(None, 'tm', ('groups', 'uv')), parts along dimension 2, may hold values from -200 to 200
- tile_owner: int32 [4, 8192, 1], P('tm', ('groups', 'uv')), parts along dimension 1, may hold values from 0 to 3; in each aligned block of 1024 rows (0 to 1023, 1024 to 2047, ..., all dimensions but the last counted through in order) at most 640 rows name the same one
- tile_cell_index: int32 [4, 8192], P('tm', ('groups', 'uv')), parts along dimension 1, may hold values from 0 to 1023
- directions: float32 [2, 1024], replicated, may hold values from -0.1 to 0.1
- sky_flux: bfloat16 [1024, 256], P(None, 'chan'), may hold values from -0.1875 to 0.1875
Outputs:
- residual: bfloat16 [2, 4, 8192, 256], P(None, 'tm', ('groups', 'uv'), 'chan'), parts along dimension 2
- dirty_grid: float32 [8, 2, 1024, 256], P(('groups', 'uv'), None, 'tm', 'chan'), parts along dimension 0
- gradient: float32 [2048, 256], P('groups', 'chan'), parts along dimension 0
The draws below stay inside these ranges and needn't reach their ends.
There are 2 independent parts, one for each index of `groups`. The reference program is written for one: setup_inputs(seed, part) draws one part's arguments, and reference() takes and returns one part's arrays. A program takes and returns all parts, laid end to end along the dimension named above; an argument that names none is the same for every part. Nothing has to cross between parts.
Inputs may be any that keep to these rules, and one draw needn't show every extreme that they name: `tile_owner`: each aligned block of 1024 entries (one dump of the baselines of one index of uv) names any tile at most 640 times; in some blocks a tile is named exactly 640 times.
All inputs are finite; a program needn't handle non-finite values. No bound on the sum of `baseline_keep_mask` or of `channel_flags` on one device may be relied on, other than what follows from the above.
Results may differ from the reference program's by a relative error of at most 0.008.
Values may be sent and summed in bfloat16 or wider, within the bound.
A program may use at most 64 MiB of HBM per device.

```python
import math
import jax
import jax.numpy as jnp
import numpy as np
from jax import lax

NCOMP = 1024
CH = 256
CELLS = 1024
BL_DEV = 1024
BASE = 4096
DUMPS = 4
TILES = 4
MOST = 640


def touch_ends(result, key, low, top_value):
    spot = [jax.random.randint(jax.random.fold_in(key, axis), (), 0, length) for axis, length in enumerate(result.shape)]
    widest = result.shape.index(max(result.shape))
    neighbour = spot[:widest] + [(spot[widest] + 1) % result.shape[widest]] + spot[widest + 1:]
    return result.at[tuple(spot)].set(low).at[tuple(neighbour)].set(top_value)


def steps_of(key, dims, shards, least, high):
    gain, own = 1.0, jax.random.fold_in(key, 6)
    for position, shards_of in shards:
        heights = jnp.exp(jax.random.uniform(jax.random.fold_in(own, position), (shards_of,), jnp.float32, least / len(shards), high / len(shards)))
        gain = gain * jnp.repeat(heights, dims[position] // shards_of).reshape([-1 if axis == position else 1 for axis in range(len(dims))])
    return gain


def routed_block(key, own, number, rows, amount, top, most, lean):
    ranking = jax.random.permutation(key, amount)
    heavy_load, usual = portions_of(amount, rows * top, most, lean, True), portions_of(amount, rows * top, most, lean, False)
    places = jnp.arange(amount)

    def named(sizes, offset_by):
        used = int((sizes > 0).sum())
        fixed = max(1, used // 4)
        shifted = fixed + (places - fixed + offset_by * (used - fixed)) % max(1, amount - fixed)
        return jnp.zeros((amount,), jnp.int32).at[ranking[jnp.where(places < fixed, places, shifted)]].set(jnp.asarray(sizes, jnp.int32))

    sizes = jnp.where(number % 4 == 0, named(heavy_load, number // 4), named(usual, number - number // 4 - 1))
    mixed = jax.random.permutation(jax.random.fold_in(own, 3), amount)
    donor, taker = mixed[0:amount // 2 * 2:2], mixed[1:amount // 2 * 2:2]
    margin = jnp.minimum(sizes[donor] - 1, most - sizes[taker]) // 2
    margin = jnp.where((donor == ranking[0]) | (taker == ranking[0]) | (sizes[taker] == 0), 0, jnp.maximum(margin, 0))
    shifted = jax.random.randint(jax.random.fold_in(own, 4), (amount // 2,), 0, 1 << 20) % (margin + 1)
    sizes = sizes.at[donor].add(-shifted).at[taker].add(shifted)
    items = jnp.searchsorted(jnp.cumsum(sizes), jnp.arange(rows * top), side="right").astype(jnp.int32)
    grid = items.reshape(top, rows).T
    grid = grid[jax.random.permutation(jax.random.fold_in(own, 1), rows)]
    offset_by = jax.random.randint(jax.random.fold_in(own, 2), (rows, 1), 0, top)
    return jnp.take_along_axis(grid, (jnp.arange(top)[None, :] + offset_by) % top, axis=1)


def portions_of(number_of, total, most, lean, full):
    portions = [(1 << 20) // math.isqrt(standing ** lean) + 1 for standing in range(1, number_of + 1)]
    largest = most if full else min(most, max(-(-total // number_of), total * portions[0] // sum(portions)))
    least = 1 if total - largest >= number_of - 1 else 0
    given, rest = [largest] + [least] * (number_of - 1), total - largest - least * (number_of - 1)
    while rest > 0:
        free = [i for i in range(1, number_of) if given[i] < largest] or [i for i in range(1, number_of) if given[i] < most]
        whole, left = sum([portions[i] for i in free]), rest
        for i in free:
            extra = min(most - given[i], max(1, left * portions[i] // whole), rest)
            given[i] = given[i] + extra
            rest = rest - extra
    return np.array(given)


def bell_draw(key, shape, deviation, reach, shards=(), kind=jnp.bfloat16):
    drawn = deviation * jax.random.normal(key, shape, jnp.float32)
    if shards:
        drawn = drawn * steps_of(key, shape, shards, -0.22, 0.18)
    return jnp.clip(drawn, -reach, reach).astype(kind)


def setup_inputs(seed: int = 0, part: int = 0) -> dict:
    key_list = jax.random.split(jax.random.key(seed), 9)
    own_keys = jax.random.split(jax.random.fold_in(key_list[8], part), 9)
    visibilities = bell_draw(own_keys[0], (2, DUMPS, BASE, CH), 1.0, 6.0, ((1, 2), (2, 4), (3, 2)))
    baseline_keep_mask = touch_ends((jax.random.randint(own_keys[1], (BASE,), 0, 10) < 9).astype(jnp.int32), jax.random.fold_in(own_keys[1], 1), 0, 1)
    channel_flags = touch_ends((jax.random.randint(own_keys[2], (CH,), 0, 10) < 9).astype(jnp.int32), jax.random.fold_in(own_keys[2], 1), 0, 1)
    baseline_spacing = jnp.clip(jax.random.uniform(own_keys[3], (2, DUMPS, BASE), jnp.float32, -200.0, 200.0) * steps_of(own_keys[3], (2, DUMPS, BASE), ((1, 2), (2, 4)), -0.4, 0.0), -200.0, 200.0)
    tile_owner_keys = jax.random.split(jax.random.fold_in(own_keys[4], 1), DUMPS * BASE // BL_DEV)
    tile_owner_turns = jax.random.permutation(jax.random.fold_in(own_keys[4], 3), DUMPS * BASE // BL_DEV)
    tile_owner = jax.vmap(lambda own, number: routed_block(jax.random.fold_in(own_keys[4], 2), own, number, BL_DEV, TILES, 1, MOST, 2))(tile_owner_keys, tile_owner_turns).reshape((DUMPS, BASE, 1))
    tile_cell_index = touch_ends(jax.random.randint(own_keys[5], (DUMPS, BASE), 0, CELLS), jax.random.fold_in(own_keys[5], 1), 0, CELLS - 1).astype(jnp.int32)
    directions = jnp.clip(jax.random.uniform(key_list[6], (2, NCOMP), jnp.float32, -0.1, 0.1), -0.1, 0.1)
    sky_flux = bell_draw(key_list[7], (NCOMP, CH), NCOMP ** -0.5, 0.1875, ((1, 2),))
    return dict(visibilities=visibilities, baseline_keep_mask=baseline_keep_mask, channel_flags=channel_flags, baseline_spacing=baseline_spacing, tile_owner=tile_owner, tile_cell_index=tile_cell_index, directions=directions, sky_flux=sky_flux)


TWO_PI = 2.0 * math.pi

def reference(visibilities, baseline_keep_mask, channel_flags, baseline_spacing, tile_owner, tile_cell_index, directions, sky_flux):
    row_total = DUMPS * BASE
    observed = visibilities.reshape(2, row_total, CH).astype(jnp.float32)
    spacing = baseline_spacing.reshape(2, row_total)
    row_flags = jnp.broadcast_to(baseline_keep_mask[None, :], (DUMPS, BASE)).reshape(row_total).astype(jnp.float32)
    chan_flags = channel_flags.astype(jnp.float32)
    fluxes = sky_flux.astype(jnp.float32)
    block_rows = math.gcd(row_total, 4096)
    block_count = row_total // block_rows

    def one_block(carry, block_index):
        start_row = block_index * block_rows
        rows_spacing = lax.dynamic_slice_in_dim(spacing, start_row, block_rows, 1)
        turns = rows_spacing[0][:, None] * directions[0][None, :] + rows_spacing[1][:, None] * directions[1][None, :]
        angle = turns * TWO_PI
        cosine = lax.optimization_barrier(jnp.cos(angle).astype(jnp.bfloat16)).astype(jnp.float32)
        sine = lax.optimization_barrier(jnp.sin(angle).astype(jnp.bfloat16)).astype(jnp.float32)
        model_real = jnp.dot(cosine, fluxes, preferred_element_type=jnp.float32)
        model_imag = -jnp.dot(sine, fluxes, preferred_element_type=jnp.float32)
        seen = lax.dynamic_slice_in_dim(observed, start_row, block_rows, 1)
        weights = lax.dynamic_slice_in_dim(row_flags, start_row, block_rows, 0)[:, None] * chan_flags[None, :]
        resid_real = lax.optimization_barrier(((seen[0] - model_real) * weights).astype(jnp.bfloat16))
        resid_imag = lax.optimization_barrier(((seen[1] - model_imag) * weights).astype(jnp.bfloat16))
        term = jnp.dot(cosine.T, resid_real.astype(jnp.float32), preferred_element_type=jnp.float32)
        term = term - jnp.dot(sine.T, resid_imag.astype(jnp.float32), preferred_element_type=jnp.float32)
        return (carry + term, jnp.stack([resid_real, resid_imag]))
    totals, pieces = lax.scan(one_block, jnp.zeros((NCOMP, CH), jnp.float32), jnp.arange(block_count, dtype=jnp.int32))
    residual_rows = jnp.moveaxis(pieces, 1, 0).reshape(2, row_total, CH)
    residual = residual_rows.reshape(2, DUMPS, BASE, CH)
    gradient = -(totals / math.sqrt(row_total))
    flat_index = tile_owner.reshape(row_total).astype(jnp.int32) * CELLS + tile_cell_index.reshape(row_total).astype(jnp.int32)
    row_values = jnp.moveaxis(residual_rows, 1, 0).astype(jnp.float32).reshape(row_total, 2 * CH)
    sums = jax.ops.segment_sum(row_values, flat_index, num_segments=TILES * CELLS)
    dirty_grid = sums.reshape(TILES, CELLS, 2, CH).transpose(0, 2, 1, 3)
    return (residual, dirty_grid, gradient)
```

```python
import functools
import math

import jax
import jax.numpy as jnp
from jax import lax
from jax.experimental import pallas as pl
from jax.experimental.pallas import tpu as pltpu
from jax.sharding import PartitionSpec as P

CELLS = 1024
MESH = pl.DeviceIdType.MESH

SINE = (4.442867833714977, -7.307441175438759, 3.594769894002402, -0.7843319733145079)
COSINE = (1.4142134962388915, -6.978850945949801, 5.739460314170848, -1.8835574375552104, 0.3106869568258822)


def horner(coefs, x):
    total = coefs[-1]
    for coef in coefs[-2::-1]:
        total = total * x + coef
    return total


def predict(
    spacing_ref, keep_ref, chan_ref, dirs_ref, flux_ref, seen_ref, resid_ref, grad_ref, waves, l_wide, m_wide
):
    comps = dirs_ref.shape[0]
    rows = spacing_ref.shape[1]

    @pl.when(pl.program_id(0) == 0)
    def _():
        grad_ref[...] = jnp.zeros_like(grad_ref)
        l_wide[...] = jnp.broadcast_to(dirs_ref[:, 0:1], l_wide.shape)
        m_wide[...] = jnp.broadcast_to(dirs_ref[:, 1:2], m_wide.shape)

    step = 16

    def some(index, carry):
        at = pl.ds(pl.multiple_of(index * step, step), step)
        l = l_wide[at, :]
        m = m_wide[at, :]
        for lane in range(0, rows, 128):
            u = spacing_ref[0:1, lane : lane + 128]
            v = spacing_ref[1:2, lane : lane + 128]
            turns = u * l + v * m
            x = turns - jnp.round(turns)
            square = x * x
            half_sine = horner(SINE, square) * x
            half_cosine = horner(COSINE, square)
            waves[at, lane : lane + 128] = (1.0 - half_sine * half_sine).astype(jnp.bfloat16)
            waves[at, rows + lane : rows + lane + 128] = (half_sine * half_cosine).astype(jnp.bfloat16)
        return carry

    lax.fori_loop(0, comps // step, some, 0, unroll=2)
    model = jnp.dot(flux_ref[...], waves[...], preferred_element_type=jnp.float32).T
    keep = jnp.broadcast_to(keep_ref[...], (chan_ref.shape[1], rows)).T
    weights = keep * chan_ref[...]
    real = ((seen_ref[0].astype(jnp.float32) - model[:rows]) * weights).astype(jnp.bfloat16)
    imag = ((seen_ref[1].astype(jnp.float32) + model[rows:]) * weights).astype(jnp.bfloat16)
    resid_ref[0] = real
    resid_ref[1] = imag
    grad_ref[...] += jnp.dot(
        waves[...], jnp.concatenate([real, -imag], 0), preferred_element_type=jnp.float32
    )


def exchange(
    n, times, scale,
    ids_ref, resid_ref, grad_ref, grid_ref, total_ref,
    rows_ref, out_x, in_x, out_z, in_z, gout_x, gin_x, gout_z, gin_z, joined, gsum,
    xs, xr, zs, zr, gxs, gxr, gzs, gzr, azs, azr, axs, axr,
):
    i = lax.axis_index("uv")
    j = lax.axis_index("tm")
    chans = resid_ref.shape[2]
    width = CELLS // times

    def uv(step):
        return lax.rem(i + 1 + step, n)

    def tm(step):
        return lax.rem(j + 1 + step, times)

    barrier = pltpu.get_barrier_semaphore()
    for d in range(times - 1):
        pl.semaphore_signal(barrier, inc=1, device_id={"tm": tm(d)}, device_id_type=MESH)
    for s in range(n - 1):
        pl.semaphore_signal(barrier, inc=1, device_id={"uv": uv(s)}, device_id_type=MESH)
    pl.semaphore_wait(barrier, times - 1 + n - 1)

    def remote(src, dst, send, recv, device):
        return pltpu.make_async_remote_copy(
            src_ref=src, dst_ref=dst, send_sem=send, recv_sem=recv, device_id=device, device_id_type=MESH
        )

    def grid_x(s, d):
        return remote(out_x.at[s, d], in_x.at[s, d], xs.at[s, d], xr.at[s, d], {"tm": tm(d)})

    def grid_z(s):
        return remote(out_z.at[s], in_z.at[s], zs.at[s], zr.at[s], {"uv": uv(s)})

    def grad_x(d):
        return remote(gout_x.at[d], gin_x.at[d], gxs.at[d], gxr.at[d], {"tm": tm(d)})

    def grad_z(s):
        return remote(gout_z.at[s], gin_z.at[s], gzs.at[s], gzr.at[s], {"uv": uv(s)})

    def join_z(s):
        return remote(joined.at[j, i], joined.at[j, i], azs.at[s], azr.at[s], {"uv": uv(s)})

    def join_x(d):
        return remote(joined.at[j], joined.at[j], axs.at[d], axr.at[d], {"tm": tm(d)})

    def loop(low, high, body):
        def wrapped(s, carry):
            body(s)
            return carry

        lax.fori_loop(low, high, wrapped, 0)

    for d in range(times - 1):
        gout_x[d] = grad_ref[tm(d)].astype(gout_x.dtype)
        grad_x(d).start()

    rows_ref[:, :chans] = resid_ref[0]
    rows_ref[:, chans:] = resid_ref[1]

    def picked(tile, part):
        wanted = ids_ref[...] - (tile * CELLS + part * width)
        bins = lax.broadcasted_iota(jnp.int32, (width, rows_ref.shape[0]), 0)
        picker = jnp.where(bins == wanted, 1.0, 0.0).astype(jnp.bfloat16)
        return jnp.dot(picker, rows_ref[...], preferred_element_type=jnp.float32)

    def send_part(s):
        for d in range(times - 1):
            out_x[s, d] = picked(uv(s), tm(d)).astype(jnp.bfloat16)
            grid_x(s, d).start()

    loop(0, n, send_part)

    total = grad_ref[j]
    for d in range(times - 1):
        grad_x(d).wait_recv()
        total = total + gin_x[d].astype(jnp.float32)
    gsum[...] = total

    def send_grad(s):
        gout_z[s] = gsum[uv(s)].astype(gout_z.dtype)
        grad_z(s).start()

    loop(0, n - 1, send_grad)

    def add_part(s):
        mine = picked(uv(s), j)
        for d in range(times - 1):
            grid_x(s, d).wait_recv()
            mine = mine + in_x[s, d].astype(jnp.float32)
        return mine

    def forward(s):
        out_z[s] = add_part(s).astype(jnp.bfloat16)
        grid_z(s).start()

    loop(0, 1, forward)
    gsum[0] = gsum[i]

    def add_grad(s):
        grad_z(s).wait_recv()
        gsum[0] = gsum[0] + gin_z[s].astype(jnp.float32)

    loop(0, n - 1, add_grad)
    joined[j, i] = gsum[0].astype(joined.dtype)
    loop(0, n - 1, lambda s: join_z(s).start())
    loop(1, n - 1, forward)

    def joined_from(s):
        sender = lax.rem(i + n - 1 - s, n)
        remote(joined.at[j, sender], joined.at[j, sender], azs.at[s], azr.at[s], {"uv": uv(s)}).wait_recv()

    loop(0, n - 1, joined_from)
    for d in range(times - 1):
        join_x(d).start()

    mine = add_part(n - 1)
    grid_ref[0] = mine[:, :chans]
    grid_ref[1] = mine[:, chans:]

    def add_tile(s):
        grid_z(s).wait_recv()
        arrived = in_z[s].astype(jnp.float32)
        grid_ref[0] += arrived[:, :chans]
        grid_ref[1] += arrived[:, chans:]

    loop(0, n - 1, add_tile)
    for d in range(times - 1):
        sender = lax.rem(j + times - 1 - d, times)
        remote(joined.at[sender], joined.at[sender], axs.at[d], axr.at[d], {"tm": tm(d)}).wait_recv()
    total_ref[...] = joined[...].astype(jnp.float32) * scale

    def sent_parts(s):
        for d in range(times - 1):
            grid_x(s, d).wait_send()

    def sent_rest(s):
        grad_z(s).wait_send()
        join_z(s).wait_send()
        grid_z(s).wait_send()

    loop(0, n, sent_parts)
    loop(0, n - 1, sent_rest)
    for d in range(times - 1):
        grad_x(d).wait_send()
        join_x(d).wait_send()


def shards(
    visibilities,
    baseline_keep_mask,
    channel_flags,
    baseline_spacing,
    tile_owner,
    tile_cell_index,
    directions,
    sky_flux,
):
    dumps, base, chans = visibilities.shape[1:]
    rows = dumps * base
    n = lax.axis_size("uv")
    times = lax.axis_size("tm")
    comps = directions.shape[1]
    block = math.gcd(base, 512)
    per_dump = base // block
    vmem = pltpu.CompilerParams(vmem_limit_bytes=48 << 20)
    resid, grad = pl.pallas_call(
        predict,
        grid=(rows // block,),
        in_specs=[
            pl.BlockSpec((2, block), lambda k: (0, k)),
            pl.BlockSpec((1, block), lambda k: (0, lax.rem(k, per_dump))),
            pl.BlockSpec((1, chans), lambda k: (0, 0)),
            pl.BlockSpec((comps, 2), lambda k: (0, 0)),
            pl.BlockSpec((chans, comps), lambda k: (0, 0)),
            pl.BlockSpec((2, block, chans), lambda k: (0, k, 0)),
        ],
        out_specs=[
            pl.BlockSpec((2, block, chans), lambda k: (0, k, 0)),
            pl.BlockSpec((comps, chans), lambda k: (0, 0)),
        ],
        out_shape=[
            jax.ShapeDtypeStruct((2, rows, chans), jnp.bfloat16),
            jax.ShapeDtypeStruct((comps, chans), jnp.float32),
        ],
        scratch_shapes=[
            pltpu.VMEM((comps, 2 * block), jnp.bfloat16),
            pltpu.VMEM((comps, 128), jnp.float32),
            pltpu.VMEM((comps, 128), jnp.float32),
        ],
        compiler_params=vmem,
        name="predict",
    )(
        baseline_spacing.reshape(2, rows),
        baseline_keep_mask.astype(jnp.float32).reshape(1, base),
        channel_flags.astype(jnp.float32).reshape(1, chans),
        directions.T,
        sky_flux.T,
        visibilities.reshape(2, rows, chans),
    )
    ids = tile_owner.reshape(1, rows) * CELLS + tile_cell_index.reshape(1, rows)
    width = CELLS // times
    piece = comps // (times * n)
    kind = jnp.bfloat16 if piece % 16 == 0 else jnp.float32
    dma = pltpu.SemaphoreType.DMA
    whole = pl.BlockSpec(memory_space=pltpu.VMEM)
    grid, total = pl.pallas_call(
        functools.partial(exchange, n, times, -1.0 / math.sqrt(rows * n * times)),
        in_specs=[whole] * 3,
        out_specs=[whole] * 2,
        out_shape=[
            jax.ShapeDtypeStruct((2, width, chans), jnp.float32),
            jax.ShapeDtypeStruct((times, n, piece, chans), jnp.float32),
        ],
        scratch_shapes=[
            pltpu.VMEM((rows, 2 * chans), jnp.bfloat16),
            pltpu.VMEM((n, times - 1, width, 2 * chans), jnp.bfloat16),
            pltpu.VMEM((n, times - 1, width, 2 * chans), jnp.bfloat16),
            pltpu.VMEM((n - 1, width, 2 * chans), jnp.bfloat16),
            pltpu.VMEM((n - 1, width, 2 * chans), jnp.bfloat16),
            pltpu.VMEM((times - 1, n, piece, chans), kind),
            pltpu.VMEM((times - 1, n, piece, chans), kind),
            pltpu.VMEM((n - 1, piece, chans), kind),
            pltpu.VMEM((n - 1, piece, chans), kind),
            pltpu.VMEM((times, n, piece, chans), kind),
            pltpu.VMEM((n, piece, chans), jnp.float32),
            dma((n, times - 1)),
            dma((n, times - 1)),
            dma((n - 1,)),
            dma((n - 1,)),
            dma((times - 1,)),
            dma((times - 1,)),
            dma((n - 1,)),
            dma((n - 1,)),
            dma((n - 1,)),
            dma((n - 1,)),
            dma((times - 1,)),
            dma((times - 1,)),
        ],
        compiler_params=pltpu.CompilerParams(
            collective_id=0, has_side_effects=True, vmem_limit_bytes=56 << 20
        ),
        name="exchange",
    )(ids, resid, grad.reshape(times, n, piece, chans))
    return (
        resid.reshape(2, dumps, base, chans),
        grid[None],
        total.reshape(comps, chans),
    )


def solution(mesh):
    placed = (
        P(None, "tm", ("groups", "uv"), "chan"),
        P(("groups", "uv")),
        P(("groups", "chan")),
        P(None, "tm", ("groups", "uv")),
        P("tm", ("groups", "uv"), None),
        P("tm", ("groups", "uv")),
        P(),
        P(None, "chan"),
    )
    return jax.shard_map(
        shards,
        mesh=mesh,
        in_specs=placed,
        out_specs=(
            P(None, "tm", ("groups", "uv"), "chan"),
            P(("groups", "uv"), None, "tm", "chan"),
            P("groups", "chan"),
        ),
        check_vma=False,
    )
```

```python
import functools
import math

import jax
import jax.numpy as jnp
from jax import lax
from jax.experimental import pallas as pl
from jax.experimental.pallas import tpu as pltpu
from jax.sharding import PartitionSpec as P

CELLS = 1024
MESH = pl.DeviceIdType.MESH
ROUNDER = 12582912.0

SINE = (4.442867833714977, -7.307441175438759, 3.594769894002402, -0.7843319733145079)
COSINE = (1.4142134962388915, -6.978850945949801, 5.739460314170848, -1.8835574375552104, 0.3106869568258822)


def horner(coefs, x):
    total = coefs[-1]
    for coef in coefs[-2::-1]:
        total = total * x + coef
    return total


def predict(
    spacing_ref, keep_ref, chan_ref, dirs_ref, flux_ref, seen_ref, resid_ref, grad_ref,
    waves, l_wide, m_wide, flux_turned, spacing,
):
    comps = dirs_ref.shape[1]
    rows = seen_ref.shape[1]
    base = spacing_ref.shape[2]
    chans = flux_ref.shape[1]
    block = pl.program_id(0)
    dump = lax.div(block * rows, base)
    first = lax.rem(block * rows, base)

    @pl.when(block == 0)
    def _():
        grad_ref[...] = jnp.zeros_like(grad_ref)
        l_wide[...] = jnp.broadcast_to(dirs_ref[0:1, :], (128, comps)).T
        m_wide[...] = jnp.broadcast_to(dirs_ref[1:2, :], (128, comps)).T
        flux_turned[...] = flux_ref[...].astype(jnp.float32).T.astype(jnp.bfloat16)

    here = pl.ds(pl.multiple_of(first, 128), rows)
    for axis in range(2):
        row = spacing_ref[axis, 0:1, here]
        for d in range(1, spacing_ref.shape[1]):
            row = jnp.where(dump == d, spacing_ref[axis, d : d + 1, here], row)
        spacing[axis : axis + 1, :] = row
    step = 16

    def some(index, carry):
        at = pl.ds(pl.multiple_of(index * step, step), step)
        l = l_wide[at, :]
        m = m_wide[at, :]
        for lane in range(0, rows, 128):
            u = spacing[0:1, lane : lane + 128]
            v = spacing[1:2, lane : lane + 128]
            turns = u * l + v * m
            x = turns - ((turns + ROUNDER) - ROUNDER)
            square = x * x
            half_sine = horner(SINE, square) * x
            half_cosine = horner(COSINE, square)
            waves[at, lane : lane + 128] = (1.0 - half_sine * half_sine).astype(jnp.bfloat16)
            waves[at, rows + lane : rows + lane + 128] = (half_sine * half_cosine).astype(jnp.bfloat16)
        return carry

    lax.fori_loop(0, comps // step, some, 0, unroll=2)
    model = jnp.dot(flux_turned[...], waves[...], preferred_element_type=jnp.float32).T
    keep_row = keep_ref[:, here].astype(jnp.float32)
    weights = jnp.broadcast_to(keep_row, (chans, rows)).T * chan_ref[...].astype(jnp.float32)
    real = ((seen_ref[0].astype(jnp.float32) - model[:rows]) * weights).astype(jnp.bfloat16)
    imag = ((seen_ref[1].astype(jnp.float32) + model[rows:]) * weights).astype(jnp.bfloat16)
    resid_ref[0] = real
    resid_ref[1] = imag
    grad_ref[...] += jnp.dot(
        waves[...], jnp.concatenate([real, -imag], 0), preferred_element_type=jnp.float32
    )


def exchange(
    n, times, scale,
    owner_ref, cell_ref, resid_ref, grad_ref, grid_ref, total_ref,
    ids_ref, rows_ref, out_x, in_x, out_z, in_z, gout_z, gin_z, shares, joined, part_sum,
    xs, xr, zs, zr, gxs, gxr, gzs, gzr, azs, azr,
):
    i = lax.axis_index("uv")
    j = lax.axis_index("tm")
    chans = resid_ref.shape[2]
    width = CELLS // times

    def uv(step):
        return lax.rem(i + 1 + step, n)

    def tm(step):
        return lax.rem(j + 1 + step, times)

    barrier = pltpu.get_barrier_semaphore()
    for d in range(times - 1):
        pl.semaphore_signal(barrier, inc=1, device_id={"tm": tm(d)}, device_id_type=MESH)
    for s in range(n - 1):
        pl.semaphore_signal(barrier, inc=1, device_id={"uv": uv(s)}, device_id_type=MESH)
    pl.semaphore_wait(barrier, times - 1 + n - 1)

    def remote(src, dst, send, recv, device):
        return pltpu.make_async_remote_copy(
            src_ref=src, dst_ref=dst, send_sem=send, recv_sem=recv, device_id=device, device_id_type=MESH
        )

    def grid_x(s, d):
        return remote(out_x.at[s, d], in_x.at[s, d], xs.at[s, d], xr.at[s, d], {"tm": tm(d)})

    more = jnp.maximum(i, n - 1 - i) - jnp.minimum(i, n - 1 - i)

    def tile_of(s):
        turn = jnp.maximum(s - more, 0)
        far = jnp.where(s < more, jnp.maximum(i, n - 1 - i) - s, jnp.minimum(i, n - 1 - i) - turn // 2)
        upward = jnp.where(s < more, 2 * i < n - 1, turn % 2 == 0)
        return jnp.where(upward, i + far, i - far)

    def arrival(way, tile):
        return remote(out_z.at[0], in_z.at[way, tile], zs.at[0], zr.at[way, tile], {"uv": uv(0)})

    def grid_z(s):
        tile = tile_of(s)
        way = jnp.where(tile > i, 0, 1)
        to = jnp.where(tile > i, i + 1, i - 1)
        return remote(out_z.at[s], in_z.at[way, tile], zs.at[s], zr.at[way, tile], {"uv": to})

    def grad_x(d, slot):
        return remote(shares.at[slot], shares.at[slot], gxs.at[d], gxr.at[d], {"tm": tm(d)})

    def grad_z(s):
        return remote(gout_z.at[s], gin_z.at[s], gzs.at[s], gzr.at[s], {"uv": uv(s)})

    def join_z(s, slot):
        return remote(joined.at[slot], joined.at[slot], azs.at[s], azr.at[s], {"uv": uv(s)})

    def loop(low, high, body):
        def wrapped(s, carry):
            body(s)
            return carry

        lax.fori_loop(low, high, wrapped, 0)

    def send_grad(s):
        gout_z[s] = grad_ref[uv(s)].astype(gout_z.dtype)
        grad_z(s).start()

    loop(0, n - 1, send_grad)
    base = owner_ref.shape[1]
    for d in range(owner_ref.shape[0]):
        ids_ref[:, d * base : (d + 1) * base] = owner_ref[d : d + 1, :] * CELLS + cell_ref[d : d + 1, :]
    rows_ref[:, :chans] = resid_ref[0]
    rows_ref[:, chans:] = resid_ref[1]

    def picked(tile, part):
        wanted = ids_ref[...] - (tile * CELLS + part * width)
        bins = lax.broadcasted_iota(jnp.int32, (width, rows_ref.shape[0]), 0)
        picker = jnp.where(bins == wanted, 1.0, 0.0).astype(jnp.bfloat16)
        return jnp.dot(picker, rows_ref[...], preferred_element_type=jnp.float32)

    def send_part(s):
        for d in range(times - 1):
            out_x[s, d] = picked(tile_of(s), tm(d)).astype(jnp.bfloat16)
            grid_x(s, d).start()

    loop(0, n // 2, send_part)
    share = grad_ref[i]
    for s in range(n - 1):
        grad_z(s).wait_recv()
        share = share + gin_z[s].astype(jnp.float32)
    shares[j] = share.astype(shares.dtype)
    for d in range(times - 1):
        grad_x(d, j).start()
    loop(n // 2, n, send_part)

    def add_part(s):
        mine = picked(tile_of(s), j)
        for d in range(times - 1):
            grid_x(s, d).wait_recv()
            mine = mine + in_x[s, d].astype(jnp.float32)
        part_sum[...] = mine

    def add_arrival(way, tile):
        arrival(way, tile).wait_recv()
        part_sum[...] += in_z[way, tile].astype(jnp.float32)

    def forward(s):
        add_part(s)
        tile = tile_of(s)

        @pl.when((tile > i) & (i > 0))
        def _():
            add_arrival(0, tile)

        @pl.when((tile < i) & (i < n - 1))
        def _():
            add_arrival(1, tile)

        out_z[s] = part_sum[...].astype(jnp.bfloat16)
        grid_z(s).start()

    loop(0, n - 2, forward)
    for d in range(times - 1):
        grad_x(d, lax.rem(j + times - 1 - d, times)).wait_recv()
    joined[i] = functools.reduce(
        lambda total, t: total + shares[t].astype(jnp.float32),
        range(1, times),
        shares[0].astype(jnp.float32),
    ).astype(joined.dtype)
    loop(0, n - 1, lambda s: join_z(s, i).start())
    loop(n - 2, n - 1, forward)
    add_part(n - 1)

    @pl.when(i > 0)
    def _():
        add_arrival(0, i)

    @pl.when(i < n - 1)
    def _():
        add_arrival(1, i)

    grid_ref[0] = part_sum[:, :chans]
    grid_ref[1] = part_sum[:, chans:]
    loop(0, n - 1, lambda s: join_z(s, lax.rem(i + n - 1 - s, n)).wait_recv())
    total_ref[...] = joined[...].astype(jnp.float32) * scale

    def sent_parts(s):
        for d in range(times - 1):
            grid_x(s, d).wait_send()

    def sent_rest(s):
        grad_z(s).wait_send()
        join_z(s, i).wait_send()
        grid_z(s).wait_send()

    loop(0, n, sent_parts)
    loop(0, n - 1, sent_rest)
    for d in range(times - 1):
        grad_x(d, j).wait_send()


def shards(
    visibilities,
    baseline_keep_mask,
    channel_flags,
    baseline_spacing,
    tile_owner,
    tile_cell_index,
    directions,
    sky_flux,
):
    dumps, base, chans = visibilities.shape[1:]
    rows = dumps * base
    n = lax.axis_size("uv")
    times = lax.axis_size("tm")
    comps = directions.shape[1]
    block = math.gcd(base, 512)
    vmem = pltpu.CompilerParams(vmem_limit_bytes=60 << 20)
    resid, grad = pl.pallas_call(
        predict,
        grid=(rows // block,),
        in_specs=[
            pl.BlockSpec((2, dumps, base), lambda k: (0, 0, 0)),
            pl.BlockSpec((1, base), lambda k: (0, 0)),
            pl.BlockSpec((1, chans), lambda k: (0, 0)),
            pl.BlockSpec((2, comps), lambda k: (0, 0)),
            pl.BlockSpec((comps, chans), lambda k: (0, 0)),
            pl.BlockSpec((2, block, chans), lambda k: (0, k, 0)),
        ],
        out_specs=[
            pl.BlockSpec((2, block, chans), lambda k: (0, k, 0)),
            pl.BlockSpec((comps, chans), lambda k: (0, 0)),
        ],
        out_shape=[
            jax.ShapeDtypeStruct((2, rows, chans), jnp.bfloat16),
            jax.ShapeDtypeStruct((comps, chans), jnp.float32),
        ],
        scratch_shapes=[
            pltpu.VMEM((comps, 2 * block), jnp.bfloat16),
            pltpu.VMEM((comps, 128), jnp.float32),
            pltpu.VMEM((comps, 128), jnp.float32),
            pltpu.VMEM((chans, comps), jnp.bfloat16),
            pltpu.VMEM((2, block), jnp.float32),
        ],
        compiler_params=vmem,
        name="predict",
    )(
        baseline_spacing,
        baseline_keep_mask.reshape(1, base),
        channel_flags.reshape(1, chans),
        directions,
        sky_flux,
        visibilities.reshape(2, rows, chans),
    )
    width = CELLS // times
    piece = comps // n
    kind = jnp.bfloat16 if piece % 16 == 0 else jnp.float32
    dma = pltpu.SemaphoreType.DMA
    whole = pl.BlockSpec(memory_space=pltpu.VMEM)
    grid, total = pl.pallas_call(
        functools.partial(exchange, n, times, -1.0 / math.sqrt(rows * n * times)),
        in_specs=[whole] * 4,
        out_specs=[whole] * 2,
        out_shape=[
            jax.ShapeDtypeStruct((2, width, chans), jnp.float32),
            jax.ShapeDtypeStruct((n, piece, chans), jnp.float32),
        ],
        scratch_shapes=[
            pltpu.VMEM((1, rows), jnp.int32),
            pltpu.VMEM((rows, 2 * chans), jnp.bfloat16),
            pltpu.VMEM((n, times - 1, width, 2 * chans), jnp.bfloat16),
            pltpu.VMEM((n, times - 1, width, 2 * chans), jnp.bfloat16),
            pltpu.VMEM((n - 1, width, 2 * chans), jnp.bfloat16),
            pltpu.VMEM((2, n, width, 2 * chans), jnp.bfloat16),
            pltpu.VMEM((n - 1, piece, chans), kind),
            pltpu.VMEM((n - 1, piece, chans), kind),
            pltpu.VMEM((times, piece, chans), kind),
            pltpu.VMEM((n, piece, chans), kind),
            pltpu.VMEM((width, 2 * chans), jnp.float32),
            dma((n, times - 1)),
            dma((n, times - 1)),
            dma((n - 1,)),
            dma((2, n)),
            dma((times - 1,)),
            dma((times - 1,)),
            dma((n - 1,)),
            dma((n - 1,)),
            dma((n - 1,)),
            dma((n - 1,)),
        ],
        compiler_params=pltpu.CompilerParams(
            collective_id=0, has_side_effects=True, vmem_limit_bytes=56 << 20
        ),
        name="exchange",
    )(tile_owner.reshape(dumps, base), tile_cell_index, resid, grad.reshape(n, piece, chans))
    return (
        resid.reshape(2, dumps, base, chans),
        grid[None],
        total.reshape(comps, chans),
    )


def solution(mesh):
    placed = (
        P(None, "tm", ("groups", "uv"), "chan"),
        P(("groups", "uv")),
        P(("groups", "chan")),
        P(None, "tm", ("groups", "uv")),
        P("tm", ("groups", "uv"), None),
        P("tm", ("groups", "uv")),
        P(),
        P(None, "chan"),
    )
    return jax.shard_map(
        shards,
        mesh=mesh,
        in_specs=placed,
        out_specs=(
            P(None, "tm", ("groups", "uv"), "chan"),
            P(("groups", "uv"), None, "tm", "chan"),
            P("groups", "chan"),
        ),
        check_vma=False,
    )
```

```python
import functools
import math

import jax
import jax.numpy as jnp
from jax import lax
from jax.experimental import pallas as pl
from jax.experimental.pallas import tpu as pltpu
from jax.sharding import PartitionSpec as P

CELLS = 1024
MESH = pl.DeviceIdType.MESH
ROUNDER = 12582912.0

SINE = (4.442867833714977, -7.307441175438759, 3.594769894002402, -0.7843319733145079)
COSINE = (1.4142134962388915, -6.978850945949801, 5.739460314170848, -1.8835574375552104, 0.3106869568258822)


def horner(coefs, x):
    total = coefs[-1]
    for coef in coefs[-2::-1]:
        total = total * x + coef
    return total


def predict(
    spacing_ref, keep_ref, chan_ref, dirs_ref, flux_ref, seen_ref, resid_ref, grad_ref,
    waves, l_wide, m_wide, flux_turned, spacing,
):
    comps = dirs_ref.shape[1]
    rows = seen_ref.shape[1]
    base = spacing_ref.shape[2]
    chans = flux_ref.shape[1]
    block = pl.program_id(0)
    dump = lax.div(block * rows, base)
    first = lax.rem(block * rows, base)

    @pl.when(block == 0)
    def _():
        grad_ref[...] = jnp.zeros_like(grad_ref)
        l_wide[...] = jnp.broadcast_to(dirs_ref[0:1, :], (128, comps)).T
        m_wide[...] = jnp.broadcast_to(dirs_ref[1:2, :], (128, comps)).T
        flux_turned[...] = flux_ref[...].astype(jnp.float32).T.astype(jnp.bfloat16)

    here = pl.ds(pl.multiple_of(first, 128), rows)
    for axis in range(2):
        row = spacing_ref[axis, 0:1, here]
        for d in range(1, spacing_ref.shape[1]):
            row = jnp.where(dump == d, spacing_ref[axis, d : d + 1, here], row)
        spacing[axis : axis + 1, :] = row
    step = 16

    def some(index, carry):
        at = pl.ds(pl.multiple_of(index * step, step), step)
        l = l_wide[at, :]
        m = m_wide[at, :]
        for lane in range(0, rows, 128):
            u = spacing[0:1, lane : lane + 128]
            v = spacing[1:2, lane : lane + 128]
            turns = u * l + v * m
            x = turns - ((turns + ROUNDER) - ROUNDER)
            square = x * x
            half_sine = horner(SINE, square) * x
            half_cosine = horner(COSINE, square)
            waves[at, lane : lane + 128] = (1.0 - half_sine * half_sine).astype(jnp.bfloat16)
            waves[at, rows + lane : rows + lane + 128] = (half_sine * half_cosine).astype(jnp.bfloat16)
        return carry

    lax.fori_loop(0, comps // step, some, 0, unroll=8)
    model = jnp.dot(flux_turned[...], waves[...], preferred_element_type=jnp.float32).T
    keep_row = keep_ref[:, here].astype(jnp.float32)
    weights = jnp.broadcast_to(keep_row, (chans, rows)).T * chan_ref[...].astype(jnp.float32)
    real = ((seen_ref[0].astype(jnp.float32) - model[:rows]) * weights).astype(jnp.bfloat16)
    imag = ((seen_ref[1].astype(jnp.float32) + model[rows:]) * weights).astype(jnp.bfloat16)
    resid_ref[0] = real
    resid_ref[1] = imag
    grad_ref[...] += jnp.dot(
        waves[...], jnp.concatenate([real, -imag], 0), preferred_element_type=jnp.float32
    )


def exchange(
    n, times,
    owner_ref, cell_ref, resid_ref, grad_ref, grid_ref, total_ref,
    ids_ref, rows_ref, out_x, in_x, out_z, in_z, gout_z, gin_z, shares, joined, part_sum,
    xs, xr, zs, zr, gxs, gxr, gzs, gzr, azs, azr,
):
    i = lax.axis_index("uv")
    j = lax.axis_index("tm")
    chans = resid_ref.shape[2]
    width = CELLS // times

    def uv(step):
        return lax.rem(i + 1 + step, n)

    def tm(step):
        return lax.rem(j + 1 + step, times)

    barrier = pltpu.get_barrier_semaphore()
    for d in range(times - 1):
        pl.semaphore_signal(barrier, inc=1, device_id={"tm": tm(d)}, device_id_type=MESH)
    for s in range(n - 1):
        pl.semaphore_signal(barrier, inc=1, device_id={"uv": uv(s)}, device_id_type=MESH)
    pl.semaphore_wait(barrier, times - 1 + n - 1)

    def remote(src, dst, send, recv, device):
        return pltpu.make_async_remote_copy(
            src_ref=src, dst_ref=dst, send_sem=send, recv_sem=recv, device_id=device, device_id_type=MESH
        )

    def grid_x(s, d):
        return remote(out_x.at[s, d], in_x.at[s, d], xs.at[s, d], xr.at[s, d], {"tm": tm(d)})

    more = jnp.maximum(i, n - 1 - i) - jnp.minimum(i, n - 1 - i)

    def tile_of(s):
        turn = jnp.maximum(s - more, 0)
        far = jnp.where(s < more, jnp.maximum(i, n - 1 - i) - s, jnp.minimum(i, n - 1 - i) - turn // 2)
        upward = jnp.where(s < more, 2 * i < n - 1, turn % 2 == 0)
        return jnp.where(upward, i + far, i - far)

    def arrival(way, tile):
        return remote(out_z.at[0], in_z.at[way, tile], zs.at[0], zr.at[way, tile], {"uv": uv(0)})

    def grid_z(s):
        tile = tile_of(s)
        way = jnp.where(tile > i, 0, 1)
        to = jnp.where(tile > i, i + 1, i - 1)
        return remote(out_z.at[s], in_z.at[way, tile], zs.at[s], zr.at[way, tile], {"uv": to})

    def grad_x(d, slot):
        return remote(shares.at[slot], shares.at[slot], gxs.at[d], gxr.at[d], {"tm": tm(d)})

    def grad_z(s):
        return remote(gout_z.at[s], gin_z.at[s], gzs.at[s], gzr.at[s], {"uv": uv(s)})

    def join_z(s, slot):
        return remote(joined.at[slot], joined.at[slot], azs.at[s], azr.at[s], {"uv": uv(s)})

    def loop(low, high, body):
        def wrapped(s, carry):
            body(s)
            return carry

        lax.fori_loop(low, high, wrapped, 0)

    def send_grad(s):
        gout_z[s] = grad_ref[uv(s)].astype(gout_z.dtype)
        grad_z(s).start()

    loop(0, n - 1, send_grad)
    base = owner_ref.shape[1]
    for d in range(owner_ref.shape[0]):
        ids_ref[:, d * base : (d + 1) * base] = owner_ref[d : d + 1, :] * CELLS + cell_ref[d : d + 1, :]
    rows_ref[:, :chans] = resid_ref[0]
    rows_ref[:, chans:] = resid_ref[1]

    def picked(tile, part):
        wanted = ids_ref[...] - (tile * CELLS + part * width)
        bins = lax.broadcasted_iota(jnp.int32, (width, rows_ref.shape[0]), 0)
        picker = jnp.where(bins == wanted, 1.0, 0.0).astype(jnp.bfloat16)
        return jnp.dot(picker, rows_ref[...], preferred_element_type=jnp.float32)

    def send_part(s):
        for d in range(times - 1):
            out_x[s, d] = picked(tile_of(s), tm(d)).astype(jnp.bfloat16)
            grid_x(s, d).start()

    loop(0, n // 2, send_part)
    share = grad_ref[i]
    for s in range(n - 1):
        grad_z(s).wait_recv()
        share = share + gin_z[s].astype(jnp.float32)
    shares[j] = share.astype(shares.dtype)
    for d in range(times - 1):
        grad_x(d, j).start()
    loop(n // 2, n, send_part)

    def add_part(s):
        mine = picked(tile_of(s), j)
        for d in range(times - 1):
            grid_x(s, d).wait_recv()
            mine = mine + in_x[s, d].astype(jnp.float32)
        part_sum[...] = mine

    def add_arrival(way, tile):
        arrival(way, tile).wait_recv()
        part_sum[...] += in_z[way, tile].astype(jnp.float32)

    def forward(s):
        add_part(s)
        tile = tile_of(s)

        @pl.when((tile > i) & (i > 0))
        def _():
            add_arrival(0, tile)

        @pl.when((tile < i) & (i < n - 1))
        def _():
            add_arrival(1, tile)

        out_z[s] = part_sum[...].astype(jnp.bfloat16)
        grid_z(s).start()

    loop(0, n - 2, forward)
    for d in range(times - 1):
        grad_x(d, lax.rem(j + times - 1 - d, times)).wait_recv()
    joined[i] = functools.reduce(
        lambda total, t: total + shares[t].astype(jnp.float32),
        range(1, times),
        shares[0].astype(jnp.float32),
    ).astype(joined.dtype)
    loop(0, n - 1, lambda s: join_z(s, i).start())
    loop(n - 2, n - 1, forward)
    add_part(n - 1)

    @pl.when(i > 0)
    def _():
        add_arrival(0, i)

    @pl.when(i < n - 1)
    def _():
        add_arrival(1, i)

    grid_ref[0] = part_sum[:, :chans]
    grid_ref[1] = part_sum[:, chans:]
    loop(0, n - 1, lambda s: join_z(s, lax.rem(i + n - 1 - s, n)).wait_recv())
    total_ref[...] = joined[...]

    def sent_parts(s):
        for d in range(times - 1):
            grid_x(s, d).wait_send()

    def sent_rest(s):
        grad_z(s).wait_send()
        join_z(s, i).wait_send()
        grid_z(s).wait_send()

    loop(0, n, sent_parts)
    loop(0, n - 1, sent_rest)
    for d in range(times - 1):
        grad_x(d, j).wait_send()


def shards(
    visibilities,
    baseline_keep_mask,
    channel_flags,
    baseline_spacing,
    tile_owner,
    tile_cell_index,
    directions,
    sky_flux,
):
    dumps, base, chans = visibilities.shape[1:]
    rows = dumps * base
    n = lax.axis_size("uv")
    times = lax.axis_size("tm")
    comps = directions.shape[1]
    block = math.gcd(base, 512)
    vmem = pltpu.CompilerParams(vmem_limit_bytes=60 << 20)
    resid, grad = pl.pallas_call(
        predict,
        grid=(rows // block,),
        in_specs=[
            pl.BlockSpec((2, dumps, base), lambda k: (0, 0, 0)),
            pl.BlockSpec((1, base), lambda k: (0, 0)),
            pl.BlockSpec((1, chans), lambda k: (0, 0)),
            pl.BlockSpec((2, comps), lambda k: (0, 0)),
            pl.BlockSpec((comps, chans), lambda k: (0, 0)),
            pl.BlockSpec((2, block, chans), lambda k: (0, k, 0)),
        ],
        out_specs=[
            pl.BlockSpec((2, block, chans), lambda k: (0, k, 0)),
            pl.BlockSpec((comps, chans), lambda k: (0, 0)),
        ],
        out_shape=[
            jax.ShapeDtypeStruct((2, rows, chans), jnp.bfloat16),
            jax.ShapeDtypeStruct((comps, chans), jnp.float32),
        ],
        scratch_shapes=[
            pltpu.VMEM((comps, 2 * block), jnp.bfloat16),
            pltpu.VMEM((comps, 128), jnp.float32),
            pltpu.VMEM((comps, 128), jnp.float32),
            pltpu.VMEM((chans, comps), jnp.bfloat16),
            pltpu.VMEM((2, block), jnp.float32),
        ],
        compiler_params=vmem,
        name="predict",
    )(
        baseline_spacing,
        baseline_keep_mask.reshape(1, base),
        channel_flags.reshape(1, chans),
        directions,
        sky_flux,
        visibilities.reshape(2, rows, chans),
    )
    width = CELLS // times
    piece = comps // n
    kind = jnp.bfloat16 if piece % 16 == 0 else jnp.float32
    dma = pltpu.SemaphoreType.DMA
    whole = pl.BlockSpec(memory_space=pltpu.VMEM)
    grid, total = pl.pallas_call(
        functools.partial(exchange, n, times),
        in_specs=[whole] * 4,
        out_specs=[whole] * 2,
        out_shape=[
            jax.ShapeDtypeStruct((2, width, chans), jnp.float32),
            jax.ShapeDtypeStruct((n, piece, chans), kind),
        ],
        scratch_shapes=[
            pltpu.VMEM((1, rows), jnp.int32),
            pltpu.VMEM((rows, 2 * chans), jnp.bfloat16),
            pltpu.VMEM((n, times - 1, width, 2 * chans), jnp.bfloat16),
            pltpu.VMEM((n, times - 1, width, 2 * chans), jnp.bfloat16),
            pltpu.VMEM((n - 1, width, 2 * chans), jnp.bfloat16),
            pltpu.VMEM((2, n, width, 2 * chans), jnp.bfloat16),
            pltpu.VMEM((n - 1, piece, chans), kind),
            pltpu.VMEM((n - 1, piece, chans), kind),
            pltpu.VMEM((times, piece, chans), kind),
            pltpu.VMEM((n, piece, chans), kind),
            pltpu.VMEM((width, 2 * chans), jnp.float32),
            dma((n, times - 1)),
            dma((n, times - 1)),
            dma((n - 1,)),
            dma((2, n)),
            dma((times - 1,)),
            dma((times - 1,)),
            dma((n - 1,)),
            dma((n - 1,)),
            dma((n - 1,)),
            dma((n - 1,)),
        ],
        compiler_params=pltpu.CompilerParams(
            collective_id=0, has_side_effects=True, vmem_limit_bytes=56 << 20
        ),
        name="exchange",
    )(tile_owner.reshape(dumps, base), tile_cell_index, resid, grad.reshape(n, piece, chans))
    return (
        resid.reshape(2, dumps, base, chans),
        grid[None],
        total.reshape(comps, chans).astype(jnp.float32) * (-1.0 / math.sqrt(rows * n * times)),
    )


def solution(mesh):
    placed = (
        P(None, "tm", ("groups", "uv"), "chan"),
        P(("groups", "uv")),
        P(("groups", "chan")),
        P(None, "tm", ("groups", "uv")),
        P("tm", ("groups", "uv"), None),
        P("tm", ("groups", "uv")),
        P(),
        P(None, "chan"),
    )
    return jax.shard_map(
        shards,
        mesh=mesh,
        in_specs=placed,
        out_specs=(
            P(None, "tm", ("groups", "uv"), "chan"),
            P(("groups", "uv"), None, "tm", "chan"),
            P("groups", "chan"),
        ),
        check_vma=False,
    )
```
